512 devices in a mesh: gx: 16 (over y, z_lo), gy: 32 (over x, z_hi, core).
Axes of the slice: x: 4, y: 4, z: 16 (z_hi: 4, z_lo: 4; z = z_hi * 4 + z_lo), core: 2. Of those that a mesh axis runs over, the one named last changes fastest.
Arguments:
- impedance: bfloat16 [16, 32, 2, 1024, 1024], P('gx', 'gy'), may hold values from -0.1875 to 0.1875
- sources: bfloat16 [16, 32, 2, 48, 1024], P('gx', 'gy'), may hold values from -6 to 6
- pattern: int32 [16, 32, 2, 2], P('gx', 'gy'), may hold values from 0 to 7
Outputs:
- combined: bfloat16 [16, 32, 2, 48, 1024], P('gx', 'gy')
The draws below stay inside these ranges and needn't reach their ends.
All inputs are finite; a program needn't handle non-finite values.
Results may differ from the reference program's by a relative error of at most 0.02.
Values sent between devices are 32-bit elements; how exact they have to be, the bound alone decides.
A program may use at most 64 MiB of HBM per device.

```python
import jax
import jax.numpy as jnp
from jax import lax

M = 1024
R = 48
SUBX = 16
SUBY = 32


def with_ends(array, rng, smallest, high):
    longest = array.shape.index(max(array.shape))
    spots = []
    for shift in (0, 1):
        where = [jax.random.randint(jax.random.fold_in(rng, axis), (), 0, length) for axis, length in enumerate(array.shape)]
        where[longest] = (where[longest] + shift) % array.shape[longest]
        spots.append(tuple(where))
    return array.at[spots[0]].set(smallest).at[spots[1]].set(high)


def levels(stream_key, extent, pieces, least, high):
    loudness, own = 1.0, jax.random.fold_in(stream_key, 6)
    for axis_at, shards_of in pieces:
        heights = jnp.exp(jax.random.uniform(jax.random.fold_in(own, axis_at), (shards_of,), jnp.float32, least / len(pieces), high / len(pieces)))
        loudness = loudness * jnp.repeat(heights, extent[axis_at] // shards_of).reshape([-1 if axis == axis_at else 1 for axis in range(len(extent))])
    return loudness


def gaussian(rng, dims, scale, limit, cuts=(), kind=jnp.bfloat16):
    array = jax.random.normal(rng, dims, jnp.float32) * scale
    if len(cuts) > 0:
        array = levels(rng, dims, cuts, -0.22, 0.18) * array
    return jnp.clip(array, min=-limit, max=limit).astype(kind)


def setup_inputs(seed: int = 0) -> dict:
    seeds = jax.random.split(jax.random.key(seed), 4)
    return {
        "impedance": gaussian(seeds[0], (SUBX, SUBY, 2, M, M), M ** -0.5, 0.1875, ((0, 16), (1, 32))),
        "sources": gaussian(seeds[1], (SUBX, SUBY, 2, R, M), 1.0, 6.0, ((0, 16), (1, 32))),
        "pattern": with_ends(jax.random.randint(seeds[2], (SUBX, SUBY, 2, 2), 0, 8), jax.random.fold_in(seeds[2], 1), 0, 7).astype(jnp.int32),
    }


COUPLING = 0.5


def rotate(code, real_in, imag_in):
    conj_sign = jnp.where(code >= 4, -1.0, 1.0)
    quarter = code % 4
    cos_part = jnp.where(quarter == 0, 1.0, jnp.where(quarter == 2, -1.0, 0.0))
    sine_part = jnp.where(quarter == 1, 1.0, jnp.where(quarter == 3, -1.0, 0.0))
    imag_flip = conj_sign * imag_in
    return cos_part * real_in - sine_part * imag_flip, sine_part * real_in + cos_part * imag_flip


def apply_operator(left_in, down_in, edge_codes, operator_block, source_block, transpose):
    left_re, left_im = rotate(edge_codes[0], left_in[0], left_in[1])
    down_re, down_im = rotate(edge_codes[1], down_in[0], down_in[1])
    blended = jnp.concatenate([left_re + down_re, left_im + down_im], axis=0).astype(jnp.bfloat16)
    contract = (((1,), (1,)), ((), ())) if transpose else (((1,), (0,)), ((), ()))
    real_part = lax.dot_general(blended, operator_block[0], contract, preferred_element_type=jnp.float32)
    imag_part = lax.dot_general(blended, operator_block[1], contract, preferred_element_type=jnp.float32)
    half_rows = blended.shape[0] // 2
    out_re = real_part[:half_rows] - imag_part[half_rows:]
    out_im = imag_part[:half_rows] + real_part[half_rows:]
    return source_block.astype(jnp.float32) + COUPLING * jnp.stack([out_re, out_im])


def run_sweep(impedance, sources, pattern, direction):
    count_cols = impedance.shape[0]
    count_rows = impedance.shape[1]
    previous = jnp.zeros((count_rows, 2, R, M), jnp.float32)
    finished = [None] * count_cols
    sequence = range(count_cols) if direction == 0 else range(count_cols - 1, -1, -1)
    for col_index in sequence:
        def advance_row(state_now, inputs):
            above, operator_block, source_block, edge_codes = inputs
            update = apply_operator(above, state_now, edge_codes, operator_block, source_block, direction == 1)
            return update, update

        start_state = jnp.zeros((2, R, M), jnp.float32)
        _, row_block = lax.scan(advance_row, start_state,
                                (previous, impedance[col_index], sources[col_index], pattern[col_index, :, direction]),
                                reverse=(direction == 1))
        finished[col_index] = row_block
        previous = row_block
    return jnp.stack(finished)


def reference(impedance, sources, pattern):
    forward = run_sweep(impedance, sources, pattern, 0)
    reverse = run_sweep(impedance, sources, pattern, 1)
    return (forward + reverse).astype(jnp.bfloat16)
```

```python
import functools

import jax
import jax.numpy as jnp
from jax import lax
from jax.experimental import pallas as pl
from jax.experimental.pallas import tpu as pltpu
from jax.sharding import PartitionSpec as P

COUPLING = 0.5
ROWS = 8
MESH = pl.DeviceIdType.MESH


def coefficients(code):
    flip = jnp.where(code >= 4, -1.0, 1.0).astype(jnp.float32)
    quarter = code % 4
    cos = jnp.where(quarter == 0, 1.0, jnp.where(quarter == 2, -1.0, 0.0)).astype(jnp.float32)
    sine = jnp.where(quarter == 1, 1.0, jnp.where(quarter == 3, -1.0, 0.0)).astype(jnp.float32)
    return cos, -sine * flip, sine, cos * flip


def kernel(
    nx, ny, groups, rows,
    k_hbm, s_ref, pat_ref, out_ref,
    k_ref, src_ref, sum_ref, in_x, in_y, k_sem, send_x, send_y, recv_x, recv_y,
):
    cx = lax.axis_index("gx")
    cy = lax.axis_index("gy")
    load = pltpu.make_async_copy(k_hbm, k_ref, k_sem)
    load.start()

    has = (
        (cx > 0, cy > 0),
        (cx < nx - 1, cy < ny - 1),
    )
    barrier = pltpu.get_barrier_semaphore()
    for side, (step_x, step_y) in enumerate(((-1, -1), (1, 1))):
        @pl.when(has[side][0])
        def _():
            pl.semaphore_signal(barrier, inc=1, device_id=(cx + step_x, cy), device_id_type=MESH)

        @pl.when(has[side][1])
        def _():
            pl.semaphore_signal(barrier, inc=1, device_id=(cx, cy + step_y), device_id_type=MESH)

    zero = jnp.zeros((groups, 2, rows, k_ref.shape[2]), jnp.float32)
    for side in range(2):
        @pl.when(jnp.logical_not(has[side][0]))
        def _():
            in_x[side] = zero

        @pl.when(jnp.logical_not(has[side][1]))
        def _():
            in_y[side] = zero

    for group in range(groups):
        src_ref[group] = s_ref[:, group * rows : (group + 1) * rows, :].astype(jnp.float32)

    count = sum(jnp.where(flag, 1, 0) for pair in has for flag in pair)
    pl.semaphore_wait(barrier, count)
    load.wait()

    depth = (cx + cy, nx - 1 - cx + ny - 1 - cy)
    targets = (((cx + 1, cy), (cx, cy + 1)), ((cx - 1, cy), (cx, cy - 1)))
    turns = [[coefficients(pat_ref[side, edge]) for edge in range(2)] for side in range(2)]

    def copies(side, group):
        return (
            pltpu.make_async_remote_copy(
                src_ref=sum_ref.at[side, group], dst_ref=in_x.at[side, group],
                send_sem=send_x.at[side, group], recv_sem=recv_x.at[side, group],
                device_id=targets[side][0], device_id_type=MESH,
            ),
            pltpu.make_async_remote_copy(
                src_ref=sum_ref.at[side, group], dst_ref=in_y.at[side, group],
                send_sem=send_y.at[side, group], recv_sem=recv_y.at[side, group],
                device_id=targets[side][1], device_id_type=MESH,
            ),
        )

    def advance(side, group):
        along_x, along_y = copies(side, group)

        @pl.when(has[side][0])
        def _():
            along_x.wait_recv()

        @pl.when(has[side][1])
        def _():
            along_y.wait_recv()

        (a, b, c, d), (e, f, g, h) = turns[side]
        left_re, left_im = in_x[side, group, 0], in_x[side, group, 1]
        down_re, down_im = in_y[side, group, 0], in_y[side, group, 1]
        re = (a * left_re + b * left_im) + (e * down_re + f * down_im)
        im = (c * left_re + d * left_im) + (g * down_re + h * down_im)
        first = jnp.concatenate([re, im], axis=0).astype(jnp.bfloat16)
        second = jnp.concatenate([-im, re], axis=0).astype(jnp.bfloat16)
        contract = (((1,), (side,)), ((), ()))
        product = lax.dot_general(
            first, k_ref[0], contract, preferred_element_type=jnp.float32
        ) + lax.dot_general(second, k_ref[1], contract, preferred_element_type=jnp.float32)
        width = product.shape[1]
        sum_ref[side, group] = src_ref[group] + COUPLING * product.reshape(2, rows, width)

        @pl.when(has[1 - side][0])
        def _():
            along_x.start()

        @pl.when(has[1 - side][1])
        def _():
            along_y.start()

    def section(step, carry):
        for side in range(2):
            group = step - depth[side]

            @pl.when((group >= 0) & (group < groups))
            def _():
                advance(side, group)

        return carry

    lax.fori_loop(0, nx + ny - 1 + groups - 1, section, 0)

    for group in range(groups):
        out_ref[:, group * rows : (group + 1) * rows, :] = (
            sum_ref[0, group] + sum_ref[1, group]
        ).astype(jnp.bfloat16)

    def drain(group, carry):
        for side in range(2):
            along_x, along_y = copies(side, group)

            @pl.when(has[1 - side][0])
            def _():
                along_x.wait_send()

            @pl.when(has[1 - side][1])
            def _():
                along_y.wait_send()

        return carry

    lax.fori_loop(0, groups, drain, 0)


def per_device(nx, ny, impedance, sources, pattern):
    _, _, _, count, width = sources.shape
    rows = ROWS
    groups = count // rows
    trace = (2, groups, 2, rows, width)
    vmem = pl.BlockSpec(memory_space=pltpu.VMEM)
    result = pl.pallas_call(
        functools.partial(kernel, nx, ny, groups, rows),
        out_shape=jax.ShapeDtypeStruct((2, count, width), jnp.bfloat16),
        in_specs=[
            pl.BlockSpec(memory_space=pl.ANY),
            vmem,
            pl.BlockSpec(memory_space=pltpu.SMEM),
        ],
        out_specs=vmem,
        scratch_shapes=[
            pltpu.VMEM((2, width, width), jnp.bfloat16),
            pltpu.VMEM((groups, 2, rows, width), jnp.float32),
            pltpu.VMEM(trace, jnp.float32),
            pltpu.VMEM(trace, jnp.float32),
            pltpu.VMEM(trace, jnp.float32),
            pltpu.SemaphoreType.DMA,
            pltpu.SemaphoreType.DMA((2, groups)),
            pltpu.SemaphoreType.DMA((2, groups)),
            pltpu.SemaphoreType.DMA((2, groups)),
            pltpu.SemaphoreType.DMA((2, groups)),
        ],
        compiler_params=pltpu.CompilerParams(
            collective_id=0, has_side_effects=True, vmem_limit_bytes=48 * 1024 * 1024
        ),
    )(impedance[0, 0], sources[0, 0], pattern[0, 0])
    return result[None, None]


def solution(mesh):
    in_specs = (
        P("gx", "gy", None, None, None),
        P("gx", "gy", None, None, None),
        P("gx", "gy", None, None),
    )
    out_specs = P("gx", "gy", None, None, None)
    body = functools.partial(per_device, mesh.shape["gx"], mesh.shape["gy"])
    return jax.shard_map(body, mesh=mesh, in_specs=in_specs, out_specs=out_specs, check_vma=False)
```

```python
import functools

import jax
import jax.numpy as jnp
from jax import lax
from jax.experimental import pallas as pl
from jax.experimental.pallas import tpu as pltpu
from jax.sharding import PartitionSpec as P

COUPLING = 0.5
ROWS = 4
EARLY = 3
CROSSING = 10
WINDOW = 1
CHUNKS = 8
BLOCK = 256
MESH = pl.DeviceIdType.MESH


def coefficients(code, rows):
    flip = jnp.where(code >= 4, -1.0, 1.0).astype(jnp.float32)
    quarter = code % 4
    cos = jnp.where(quarter == 0, 1.0, jnp.where(quarter == 2, -1.0, 0.0)).astype(jnp.float32)
    sine = jnp.where(quarter == 1, 1.0, jnp.where(quarter == 3, -1.0, 0.0)).astype(jnp.float32)
    real = lax.broadcasted_iota(jnp.int32, (2 * rows, 128), 0) < rows
    return jnp.where(real, cos, cos * flip), jnp.where(real, -sine * flip, sine)


def kernel(
    nx, ny, groups, rows,
    k_hbm, s_ref, pat_ref, out_ref,
    k_ref, give_ref, take_ref, src_ref, coef_ref, sum_ref, in_x, in_y, fin_out, fin_in,
    k_sem, hand_send, hand_recv, send_x, send_y, recv_x, recv_y, fin_send, fin_recv,
):
    width = k_ref.shape[-1]
    nk = ny // 2
    cx = lax.axis_index("gx")
    cy = lax.axis_index("gy")
    ck = cy // 2
    core = cy % 2
    load = pltpu.make_async_copy(k_hbm, k_ref.at[core, 0], k_sem)
    load.start()

    last_depth = nx - 1 + 2 * (nk - 1)
    depth = (cx + 2 * ck, last_depth - cx - 2 * ck)
    step_of = (1, -1)
    has_x = (cx > 0, cx < nx - 1)
    has_y = (ck > 0, ck < nk - 1)

    def core_of(parity, side, along):
        mine = depth[side] + along
        gap = 2 * mine - last_depth
        moved = (gap > -CROSSING) & (gap < CROSSING) if side == 0 else gap < -last_depth
        return jnp.where(mine < EARLY, parity, jnp.where(moved, 0, 1))

    here = tuple(tuple(core_of(parity, side, 0) for side in range(2)) for parity in range(2))
    apart = tuple(here[0][side] != here[1][side] for side in range(2))

    barrier = pltpu.get_barrier_semaphore()
    pl.semaphore_signal(barrier, inc=1, device_id=(cx, cy + 1 - 2 * core), device_id_type=MESH)
    for side in range(2):
        back = -step_of[side]

        @pl.when(has_x[side])
        def _():
            for other in range(2):
                pl.semaphore_signal(
                    barrier, inc=1, device_id=(cx + back, 2 * ck + other), device_id_type=MESH
                )

        @pl.when(has_y[side])
        def _():
            for other in range(2):
                pl.semaphore_signal(
                    barrier, inc=1, device_id=(cx, 2 * (ck + back) + other), device_id_type=MESH
                )

    zero = jnp.zeros((groups, 2 * rows, width), jnp.float32)
    for side in range(2):
        @pl.when(jnp.logical_not(has_x[side]))
        def _():
            for parity in range(2):
                in_x[parity, side] = zero

        @pl.when(jnp.logical_not(has_y[side]))
        def _():
            in_y[side, side] = zero

        for parity in range(2):
            sum_ref[parity, side] = zero

    for side in range(2):
        for edge in range(2):
            own, swap = coefficients(pat_ref[side, edge], rows)
            coef_ref[core, side, edge, 0] = own
            coef_ref[core, side, edge, 1] = swap
    full = s_ref[...].astype(jnp.float32)
    for group in range(groups):
        part = slice(group * rows, (group + 1) * rows)
        src_ref[core, group] = jnp.concatenate([full[0, part], full[1, part]], axis=0)

    def transpose(parity):
        def block(index, carry):
            piece = index // (width // BLOCK)
            start = pl.multiple_of((index % (width // BLOCK)) * BLOCK, BLOCK)
            k_ref[parity, 1, piece, :, pl.ds(start, BLOCK)] = k_ref[
                parity, 0, piece, pl.ds(start, BLOCK), :
            ].T
            return carry

        lax.fori_loop(0, 2 * (width // BLOCK), block, 0)

    count = 1 + 2 * sum(jnp.where(flag, 1, 0) for flag in has_x + has_y)
    pl.semaphore_wait(barrier, count)

    def handover(src, dst, slot):
        return pltpu.make_async_remote_copy(
            src_ref=src, dst_ref=dst, send_sem=hand_send.at[slot], recv_sem=hand_recv.at[slot],
            device_id=(cx, 2 * ck + 1 - core), device_id_type=MESH,
        )

    chunk_rows = 2 * width // CHUNKS
    per_half = CHUNKS // 2

    def hand_parts(parity):
        return (
            handover(coef_ref.at[parity], coef_ref.at[parity], 0),
            handover(src_ref.at[parity], src_ref.at[parity], 1),
        )

    def chunk_copy(chunk):
        return handover(give_ref.at[chunk], take_ref.at[chunk], 2 + chunk)

    early = (depth[0] < EARLY, depth[1] < EARLY)
    met = (here[0][0] == 0) & jnp.logical_not(early[0]) | (here[0][1] == 0) & jnp.logical_not(early[1])
    gives = (core == 0) | met
    takes = (core == 1) | met
    turn_now = early[1] | (core == 1) & jnp.logical_not(early[0])

    @pl.when(gives)
    def _():
        for part in hand_parts(core):
            part.start()

    load.wait()

    @pl.when(turn_now)
    def _():
        transpose(core)

    def give():
        def send(chunk, carry):
            start = pl.multiple_of((chunk % per_half) * chunk_rows, chunk_rows)
            give_ref[chunk] = k_ref[
                core, 0, chunk // per_half, pl.ds(start, chunk_rows), :
            ].astype(jnp.float32)
            chunk_copy(chunk).start()
            return carry

        lax.fori_loop(0, CHUNKS, send, 0)

    def take():
        for part in hand_parts(1 - core):
            part.wait_recv()

        def receive(chunk, carry):
            chunk_copy(chunk).wait_recv()
            start = pl.multiple_of((chunk % per_half) * chunk_rows, chunk_rows)
            k_ref[1 - core, 0, chunk // per_half, pl.ds(start, chunk_rows), :] = take_ref[
                chunk
            ].astype(jnp.bfloat16)
            return carry

        lax.fori_loop(0, CHUNKS, receive, 0)

        @pl.when(jnp.where(core == 0, here[1][1], here[0][1]) == core)
        def _():
            transpose(1 - core)

        @pl.when(jnp.logical_not(turn_now) & (jnp.where(core == 0, here[0][1], here[1][1]) == core))
        def _():
            transpose(core)

    take_step = jnp.where(early[0] | early[1], min(EARLY + groups, last_depth - EARLY), 0)

    def copy_x(parity, side, group):
        step = step_of[side]
        there = core_of(parity, side, 1)
        return pltpu.make_async_remote_copy(
            src_ref=sum_ref.at[parity, side, group], dst_ref=in_x.at[parity, side, group],
            send_sem=send_x.at[parity, side, group], recv_sem=recv_x.at[parity, side, group],
            device_id=(cx + step, 2 * ck + there), device_id_type=MESH,
        )

    def copy_y(parity, side, group):
        step = step_of[side]
        if parity == side:
            target = (cx, 2 * ck + 1 - core)
        else:
            target = (cx, 2 * (ck + step) + core_of(1 - parity, side, 2))
        return pltpu.make_async_remote_copy(
            src_ref=sum_ref.at[parity, side, group], dst_ref=in_y.at[1 - parity, side, group],
            send_sem=send_y.at[parity, side, group], recv_sem=recv_y.at[1 - parity, side, group],
            device_id=target, device_id_type=MESH,
        )

    def fin_copy(group):
        return pltpu.make_async_remote_copy(
            src_ref=fin_out.at[group], dst_ref=fin_in.at[group],
            send_sem=fin_send.at[group], recv_sem=fin_recv.at[group],
            device_id=(cx, 2 * ck + 1 - core), device_id_type=MESH,
        )

    is_second = (depth[0] >= depth[1], depth[0] < depth[1])
    sends_x = (has_x[1], has_x[0])
    sends_y = (has_y[1], has_y[0])

    def exchanged(value):
        return jnp.concatenate([value[rows:], value[:rows]], axis=0)

    def wide(tile):
        return jnp.concatenate([tile] * (width // 128), axis=1)

    def advance(parity, side, group):
        to_x = copy_x(parity, side, group)
        to_y = copy_y(parity, side, group)
        from_y = copy_y(1 - parity, side, group)
        first = parity == side

        @pl.when(has_x[side])
        def _():
            to_x.wait_recv()

        @pl.when(has_y[side] if first else apart[side])
        def _():
            from_y.wait_recv()

        left = in_x[parity, side, group]
        down = in_y[parity, side, group]
        coef = [[wide(coef_ref[parity, side, edge, i]) for i in range(2)] for edge in range(2)]
        blend = (
            (coef[0][0] * left + coef[0][1] * exchanged(left))
            + (coef[1][0] * down + coef[1][1] * exchanged(down))
        )
        real = lax.broadcasted_iota(jnp.int32, blend.shape, 0) < rows
        other = exchanged(blend)
        turned = jnp.where(real, -other, other)
        contract = (((1,), (0,)), ((), ()))
        product = lax.dot_general(
            blend.astype(jnp.bfloat16), k_ref[parity, side, 0], contract,
            preferred_element_type=jnp.float32,
        ) + lax.dot_general(
            turned.astype(jnp.bfloat16), k_ref[parity, side, 1], contract,
            preferred_element_type=jnp.float32,
        )
        update = src_ref[parity, group] + COUPLING * product
        sum_ref[parity, side, group] = update

        @pl.when(apart[side] if first else sends_y[side])
        def _():
            if WINDOW < groups:
                @pl.when(group >= WINDOW)
                def _():
                    copy_y(parity, side, group - WINDOW).wait_send()

            to_y.start()

        @pl.when(sends_x[side])
        def _():
            if WINDOW < groups:
                @pl.when(group >= WINDOW)
                def _():
                    copy_x(parity, side, group - WINDOW).wait_send()

            to_x.start()

        if first:
            @pl.when(jnp.logical_not(apart[side]))
            def _():
                in_y[1 - parity, side, group] = update

        last = is_second[side] | (here[parity][1 - side] != core)

        @pl.when((core != parity) & last)
        def _():
            fin_out[group] = sum_ref[parity, 0, group] + sum_ref[parity, 1, group]
            fin_copy(group).start()

    def runs(parity, side):
        return core == here[parity][side]

    def section(step, carry):
        @pl.when(gives & (step == take_step))
        def _():
            give()

        @pl.when(takes & (step == take_step))
        def _():
            take()

        for side in (1, 0):
            group = step - depth[side]
            for parity in (side, 1 - side):
                @pl.when((group >= 0) & (group < groups) & runs(parity, side))
                def _():
                    advance(parity, side, group)

        return carry

    lax.fori_loop(0, last_depth + groups, section, 0)

    def store(parts):
        for half in range(2):
            out_ref[half] = jnp.concatenate(
                [part[half * rows : (half + 1) * rows] for part in parts], axis=0
            ).astype(jnp.bfloat16)

    def any_of(parity, where):
        return (here[parity][0] == where) | (here[parity][1] == where)

    for parity in range(2):
        awaits = any_of(parity, 1 - parity)

        @pl.when((core == parity) & awaits)
        def _():
            for group in range(groups):
                fin_copy(group).wait_recv()
            store([
                fin_in[group] + sum_ref[parity, 0, group] + sum_ref[parity, 1, group]
                for group in range(groups)
            ])

        @pl.when((core == parity) & jnp.logical_not(awaits))
        def _():
            store([sum_ref[parity, 0, group] + sum_ref[parity, 1, group] for group in range(groups)])

        @pl.when((core != parity) & awaits)
        def _():
            def sent(group, carry):
                fin_copy(group).wait_send()
                return carry

            lax.fori_loop(0, groups, sent, 0)

    @pl.when(gives)
    def _():
        for part in hand_parts(core):
            part.wait_send()

        def sent(chunk, carry):
            chunk_copy(chunk).wait_send()
            return carry

        lax.fori_loop(0, CHUNKS, sent, 0)

    def drain(group, carry):
        for side in range(2):
            for parity in range(2):
                @pl.when(runs(parity, side) & sends_x[side])
                def _():
                    copy_x(parity, side, group).wait_send()

                over = apart[side] if parity == side else sends_y[side]

                @pl.when(runs(parity, side) & over)
                def _():
                    copy_y(parity, side, group).wait_send()

        return carry

    lax.fori_loop(max(0, groups - WINDOW), groups, drain, 0)


def per_device(nx, ny, impedance, sources, pattern):
    _, _, _, count, width = sources.shape
    rows = ROWS
    groups = count // rows
    trace = (2, 2, groups, 2 * rows, width)
    vmem = pl.BlockSpec(memory_space=pltpu.VMEM)
    dma = pltpu.SemaphoreType.DMA
    result = pl.pallas_call(
        functools.partial(kernel, nx, ny, groups, rows),
        out_shape=jax.ShapeDtypeStruct((2, count, width), jnp.bfloat16),
        in_specs=[
            pl.BlockSpec(memory_space=pl.ANY),
            vmem,
            pl.BlockSpec(memory_space=pltpu.SMEM),
        ],
        out_specs=vmem,
        scratch_shapes=[
            pltpu.VMEM((2, 2, 2, width, width), jnp.bfloat16),
            pltpu.VMEM((CHUNKS, 2 * width // CHUNKS, width), jnp.float32),
            pltpu.VMEM((CHUNKS, 2 * width // CHUNKS, width), jnp.float32),
            pltpu.VMEM((2, groups, 2 * rows, width), jnp.float32),
            pltpu.VMEM((2, 2, 2, 2, 2 * rows, 128), jnp.float32),
            pltpu.VMEM(trace, jnp.float32),
            pltpu.VMEM(trace, jnp.float32),
            pltpu.VMEM(trace, jnp.float32),
            pltpu.VMEM((groups, 2 * rows, width), jnp.float32),
            pltpu.VMEM((groups, 2 * rows, width), jnp.float32),
            dma,
            dma((2 + CHUNKS,)),
            dma((2 + CHUNKS,)),
            dma((2, 2, groups)),
            dma((2, 2, groups)),
            dma((2, 2, groups)),
            dma((2, 2, groups)),
            dma((groups,)),
            dma((groups,)),
        ],
        compiler_params=pltpu.CompilerParams(
            collective_id=0, has_side_effects=True, vmem_limit_bytes=56 * 1024 * 1024
        ),
    )(impedance[0, 0], sources[0, 0], pattern[0, 0])
    return result[None, None]


def solution(mesh):
    in_specs = (
        P("gx", "gy", None, None, None),
        P("gx", "gy", None, None, None),
        P("gx", "gy", None, None),
    )
    out_specs = P("gx", "gy", None, None, None)
    body = functools.partial(per_device, mesh.shape["gx"], mesh.shape["gy"])
    return jax.shard_map(body, mesh=mesh, in_specs=in_specs, out_specs=out_specs, check_vma=False)
```

```python
import functools

import jax
import jax.numpy as jnp
from jax import lax
from jax.experimental import pallas as pl
from jax.experimental.pallas import tpu as pltpu
from jax.sharding import PartitionSpec as P

COUPLING = 0.5
ROWS = 4
EARLY = 3
CROSSING = 10
WINDOW = 1
CHUNKS = 8
PIECES = 2
BLOCK = 256
MESH = pl.DeviceIdType.MESH


def coefficients(code, rows):
    flip = jnp.where(code >= 4, -1.0, 1.0).astype(jnp.float32)
    quarter = code % 4
    cos = jnp.where(quarter == 0, 1.0, jnp.where(quarter == 2, -1.0, 0.0)).astype(jnp.float32)
    sine = jnp.where(quarter == 1, 1.0, jnp.where(quarter == 3, -1.0, 0.0)).astype(jnp.float32)
    real = lax.broadcasted_iota(jnp.int32, (2 * rows, 128), 0) < rows
    return jnp.where(real, cos, cos * flip), jnp.where(real, -sine * flip, sine)


def kernel(
    nx, ny, groups, rows,
    k_hbm, s_hbm, pat_ref, out_ref,
    s_ref, k_ref, give_ref, take_ref, src_ref, coef_ref, sum_ref, in_x, in_y, fin_out, fin_in,
    s_sem, k_sem, hand_send, hand_recv, send_x, send_y, recv_x, recv_y, fin_send, fin_recv,
):
    width = k_ref.shape[-1]
    nk = ny // 2
    cx = lax.axis_index("gx")
    cy = lax.axis_index("gy")
    ck = cy // 2
    core = cy % 2
    load = pltpu.make_async_copy(k_hbm, k_ref.at[core, 0], k_sem)
    load.start()
    load_s = pltpu.make_async_copy(s_hbm, s_ref, s_sem)
    load_s.start()

    last_depth = nx - 1 + 2 * (nk - 1)
    depth = (cx + 2 * ck, last_depth - cx - 2 * ck)
    step_of = (1, -1)
    has_x = (cx > 0, cx < nx - 1)
    has_y = (ck > 0, ck < nk - 1)

    def core_of(parity, side, along):
        mine = depth[side] + along
        gap = 2 * mine - last_depth
        moved = (gap > -CROSSING) & (gap < CROSSING) if side == 0 else gap < -last_depth
        return jnp.where(mine < EARLY, parity, jnp.where(moved, 0, 1))

    here = tuple(tuple(core_of(parity, side, 0) for side in range(2)) for parity in range(2))
    apart = tuple(here[0][side] != here[1][side] for side in range(2))

    barrier = pltpu.get_barrier_semaphore()
    pl.semaphore_signal(barrier, inc=1, device_id=(cx, cy + 1 - 2 * core), device_id_type=MESH)
    for side in range(2):
        back = -step_of[side]

        @pl.when(has_x[side])
        def _():
            for other in range(2):
                pl.semaphore_signal(
                    barrier, inc=1, device_id=(cx + back, 2 * ck + other), device_id_type=MESH
                )

        @pl.when(has_y[side])
        def _():
            for other in range(2):
                pl.semaphore_signal(
                    barrier, inc=1, device_id=(cx, 2 * (ck + back) + other), device_id_type=MESH
                )

    zero = jnp.zeros((groups, 2 * rows, width), jnp.float32)
    for side in range(2):
        @pl.when(jnp.logical_not(has_x[side]))
        def _():
            for parity in range(2):
                in_x[parity, side] = zero

        @pl.when(jnp.logical_not(has_y[side]))
        def _():
            in_y[side, side] = zero

        for parity in range(2):
            sum_ref[parity, side] = zero

    for side in range(2):
        for edge in range(2):
            own, swap = coefficients(pat_ref[side, edge], rows)
            coef_ref[core, side, edge, 0] = own
            coef_ref[core, side, edge, 1] = swap
    load_s.wait()
    full = s_ref[...].astype(jnp.float32)
    for group in range(groups):
        part = slice(group * rows, (group + 1) * rows)
        src_ref[core, group] = jnp.concatenate([full[0, part], full[1, part]], axis=0)

    def transpose(parity):
        def block(index, carry):
            piece = index // (width // BLOCK)
            start = pl.multiple_of((index % (width // BLOCK)) * BLOCK, BLOCK)
            k_ref[parity, 1, piece, :, pl.ds(start, BLOCK)] = k_ref[
                parity, 0, piece, pl.ds(start, BLOCK), :
            ].T
            return carry

        lax.fori_loop(0, 2 * (width // BLOCK), block, 0)

    count = 1 + 2 * sum(jnp.where(flag, 1, 0) for flag in has_x + has_y)
    pl.semaphore_wait(barrier, count)

    def handover(src, dst, slot):
        return pltpu.make_async_remote_copy(
            src_ref=src, dst_ref=dst, send_sem=hand_send.at[slot], recv_sem=hand_recv.at[slot],
            device_id=(cx, 2 * ck + 1 - core), device_id_type=MESH,
        )

    chunk_rows = 2 * width // CHUNKS
    per_half = CHUNKS // 2

    def hand_parts(parity):
        return (
            handover(coef_ref.at[parity], coef_ref.at[parity], 0),
            handover(src_ref.at[parity], src_ref.at[parity], 1),
        )

    def chunk_copy(chunk):
        return handover(give_ref.at[chunk], take_ref.at[chunk], 2 + chunk)

    early = (depth[0] < EARLY, depth[1] < EARLY)
    met = (here[0][0] == 0) & jnp.logical_not(early[0]) | (here[0][1] == 0) & jnp.logical_not(early[1])
    gives = (core == 0) | met
    takes = (core == 1) | met
    turn_now = early[1] | (core == 1) & jnp.logical_not(early[0])

    @pl.when(gives)
    def _():
        for part in hand_parts(core):
            part.start()

    load.wait()

    @pl.when(turn_now)
    def _():
        transpose(core)

    def give():
        def send(chunk, carry):
            start = pl.multiple_of((chunk % per_half) * chunk_rows, chunk_rows)
            give_ref[chunk] = k_ref[
                core, 0, chunk // per_half, pl.ds(start, chunk_rows), :
            ].astype(jnp.float32)
            chunk_copy(chunk).start()
            return carry

        lax.fori_loop(0, CHUNKS, send, 0)

    def take():
        for part in hand_parts(1 - core):
            part.wait_recv()

        def receive(chunk, carry):
            chunk_copy(chunk).wait_recv()
            start = pl.multiple_of((chunk % per_half) * chunk_rows, chunk_rows)
            k_ref[1 - core, 0, chunk // per_half, pl.ds(start, chunk_rows), :] = take_ref[
                chunk
            ].astype(jnp.bfloat16)
            return carry

        lax.fori_loop(0, CHUNKS, receive, 0)

        @pl.when(jnp.where(core == 0, here[1][1], here[0][1]) == core)
        def _():
            transpose(1 - core)

        @pl.when(jnp.logical_not(turn_now) & (jnp.where(core == 0, here[0][1], here[1][1]) == core))
        def _():
            transpose(core)

    take_step = jnp.where(early[0] | early[1], min(EARLY + groups, last_depth - EARLY), 0)

    piece_width = width // PIECES

    def columns(piece):
        return slice(piece * piece_width, (piece + 1) * piece_width)

    def copy_x(parity, side, group, piece):
        step = step_of[side]
        there = core_of(parity, side, 1)
        slot = group * PIECES + piece
        cut = columns(piece)
        return pltpu.make_async_remote_copy(
            src_ref=sum_ref.at[parity, side, group, :, cut],
            dst_ref=in_x.at[parity, side, group, :, cut],
            send_sem=send_x.at[parity, side, slot], recv_sem=recv_x.at[parity, side, slot],
            device_id=(cx + step, 2 * ck + there), device_id_type=MESH,
        )

    def copy_y(parity, side, group, piece):
        step = step_of[side]
        if parity == side:
            target = (cx, 2 * ck + 1 - core)
        else:
            target = (cx, 2 * (ck + step) + core_of(1 - parity, side, 2))
        slot = group * PIECES + piece
        cut = columns(piece)
        return pltpu.make_async_remote_copy(
            src_ref=sum_ref.at[parity, side, group, :, cut],
            dst_ref=in_y.at[1 - parity, side, group, :, cut],
            send_sem=send_y.at[parity, side, slot], recv_sem=recv_y.at[1 - parity, side, slot],
            device_id=target, device_id_type=MESH,
        )

    def fin_copy(group):
        return pltpu.make_async_remote_copy(
            src_ref=fin_out.at[group], dst_ref=fin_in.at[group],
            send_sem=fin_send.at[group], recv_sem=fin_recv.at[group],
            device_id=(cx, 2 * ck + 1 - core), device_id_type=MESH,
        )

    is_second = (depth[0] >= depth[1], depth[0] < depth[1])
    sends_x = (has_x[1], has_x[0])
    sends_y = (has_y[1], has_y[0])

    def exchanged(value):
        return jnp.concatenate([value[rows:], value[:rows]], axis=0)

    def wide(tile):
        return jnp.concatenate([tile] * (piece_width // 128), axis=1)

    def blended(parity, side, group, piece):
        @pl.when(has_x[side])
        def _():
            copy_x(parity, side, group, piece).wait_recv()

        @pl.when(has_y[side] if parity == side else apart[side])
        def _():
            copy_y(1 - parity, side, group, piece).wait_recv()

        left = in_x[parity, side, group, :, columns(piece)]
        down = in_y[parity, side, group, :, columns(piece)]
        coef = [[wide(coef_ref[parity, side, edge, i]) for i in range(2)] for edge in range(2)]
        blend = (
            (coef[0][0] * left + coef[0][1] * exchanged(left))
            + (coef[1][0] * down + coef[1][1] * exchanged(down))
        )
        real = lax.broadcasted_iota(jnp.int32, blend.shape, 0) < rows
        other = exchanged(blend)
        turned = jnp.where(real, -other, other)
        return blend.astype(jnp.bfloat16), turned.astype(jnp.bfloat16)

    def product(parity, side, factors, piece, cut):
        contract = (((1,), (0,)), ((), ()))
        terms = [
            lax.dot_general(
                factor, k_ref[parity, side, half, columns(piece), cut], contract,
                preferred_element_type=jnp.float32,
            )
            for half, factor in enumerate(factors)
        ]
        return terms[0] + terms[1]

    def launch(parity, side, group, piece):
        first = parity == side
        for wanted, copy in (
            (apart[side] if first else sends_y[side], copy_y), (sends_x[side], copy_x)
        ):
            @pl.when(wanted)
            def _():
                if WINDOW < groups:
                    @pl.when(group >= WINDOW)
                    def _():
                        copy(parity, side, group - WINDOW, piece).wait_send()

                copy(parity, side, group, piece).start()

    def advance(parity, side, group):
        first = parity == side
        total = None
        for piece in range(PIECES - 1):
            factors = blended(parity, side, group, piece)
            term = product(parity, side, factors, piece, slice(0, width))
            total = term if total is None else total + term
        factors = blended(parity, side, group, PIECES - 1)
        for piece in range(PIECES):
            cut = columns(piece)
            term = product(parity, side, factors, PIECES - 1, cut)
            if total is not None:
                term = total[:, cut] + term
            update = src_ref[parity, group, :, cut] + COUPLING * term
            sum_ref[parity, side, group, :, cut] = update
            launch(parity, side, group, piece)
            if first:
                @pl.when(jnp.logical_not(apart[side]))
                def _():
                    in_y[1 - parity, side, group, :, cut] = update

        last = is_second[side] | (here[parity][1 - side] != core)

        @pl.when((core != parity) & last)
        def _():
            fin_out[group] = sum_ref[parity, 0, group] + sum_ref[parity, 1, group]
            fin_copy(group).start()

    def runs(parity, side):
        return core == here[parity][side]

    def section(step, carry):
        @pl.when(gives & (step == take_step))
        def _():
            give()

        @pl.when(takes & (step == take_step))
        def _():
            take()

        for side in (1, 0):
            group = step - depth[side]
            for parity in (side, 1 - side):
                @pl.when((group >= 0) & (group < groups) & runs(parity, side))
                def _():
                    advance(parity, side, group)

        return carry

    lax.fori_loop(0, last_depth + groups, section, 0)

    def store(parts):
        for half in range(2):
            out_ref[half] = jnp.concatenate(
                [part[half * rows : (half + 1) * rows] for part in parts], axis=0
            ).astype(jnp.bfloat16)

    def any_of(parity, where):
        return (here[parity][0] == where) | (here[parity][1] == where)

    for parity in range(2):
        awaits = any_of(parity, 1 - parity)

        @pl.when((core == parity) & awaits)
        def _():
            for group in range(groups):
                fin_copy(group).wait_recv()
            store([
                fin_in[group] + sum_ref[parity, 0, group] + sum_ref[parity, 1, group]
                for group in range(groups)
            ])

        @pl.when((core == parity) & jnp.logical_not(awaits))
        def _():
            store([sum_ref[parity, 0, group] + sum_ref[parity, 1, group] for group in range(groups)])

        @pl.when((core != parity) & awaits)
        def _():
            def sent(group, carry):
                fin_copy(group).wait_send()
                return carry

            lax.fori_loop(0, groups, sent, 0)

    @pl.when(gives)
    def _():
        for part in hand_parts(core):
            part.wait_send()

        def sent(chunk, carry):
            chunk_copy(chunk).wait_send()
            return carry

        lax.fori_loop(0, CHUNKS, sent, 0)

    def drain(group, carry):
        for side in range(2):
            for parity in range(2):
                over = apart[side] if parity == side else sends_y[side]
                for piece in range(PIECES):
                    @pl.when(runs(parity, side) & sends_x[side])
                    def _():
                        copy_x(parity, side, group, piece).wait_send()

                    @pl.when(runs(parity, side) & over)
                    def _():
                        copy_y(parity, side, group, piece).wait_send()

        return carry

    lax.fori_loop(max(0, groups - WINDOW), groups, drain, 0)


def per_device(nx, ny, impedance, sources, pattern):
    _, _, _, count, width = sources.shape
    rows = ROWS
    groups = count // rows
    trace = (2, 2, groups, 2 * rows, width)
    vmem = pl.BlockSpec(memory_space=pltpu.VMEM)
    dma = pltpu.SemaphoreType.DMA
    result = pl.pallas_call(
        functools.partial(kernel, nx, ny, groups, rows),
        out_shape=jax.ShapeDtypeStruct((2, count, width), jnp.bfloat16),
        in_specs=[
            pl.BlockSpec(memory_space=pl.ANY),
            pl.BlockSpec(memory_space=pl.ANY),
            pl.BlockSpec(memory_space=pltpu.SMEM),
        ],
        out_specs=vmem,
        scratch_shapes=[
            pltpu.VMEM((2, count, width), jnp.bfloat16),
            pltpu.VMEM((2, 2, 2, width, width), jnp.bfloat16),
            pltpu.VMEM((CHUNKS, 2 * width // CHUNKS, width), jnp.float32),
            pltpu.VMEM((CHUNKS, 2 * width // CHUNKS, width), jnp.float32),
            pltpu.VMEM((2, groups, 2 * rows, width), jnp.float32),
            pltpu.VMEM((2, 2, 2, 2, 2 * rows, 128), jnp.float32),
            pltpu.VMEM(trace, jnp.float32),
            pltpu.VMEM(trace, jnp.float32),
            pltpu.VMEM(trace, jnp.float32),
            pltpu.VMEM((groups, 2 * rows, width), jnp.float32),
            pltpu.VMEM((groups, 2 * rows, width), jnp.float32),
            dma,
            dma,
            dma((2 + CHUNKS,)),
            dma((2 + CHUNKS,)),
            dma((2, 2, groups * PIECES)),
            dma((2, 2, groups * PIECES)),
            dma((2, 2, groups * PIECES)),
            dma((2, 2, groups * PIECES)),
            dma((groups,)),
            dma((groups,)),
        ],
        compiler_params=pltpu.CompilerParams(
            collective_id=0, has_side_effects=True, vmem_limit_bytes=56 * 1024 * 1024
        ),
    )(impedance[0, 0], sources[0, 0], pattern[0, 0])
    return result[None, None]


def solution(mesh):
    in_specs = (
        P("gx", "gy", None, None, None),
        P("gx", "gy", None, None, None),
        P("gx", "gy", None, None),
    )
    out_specs = P("gx", "gy", None, None, None)
    body = functools.partial(per_device, mesh.shape["gx"], mesh.shape["gy"])
    return jax.shard_map(body, mesh=mesh, in_specs=in_specs, out_specs=out_specs, check_vma=False)
```

```python
import functools

import jax
import jax.numpy as jnp
from jax import lax
from jax.experimental import pallas as pl
from jax.experimental.pallas import tpu as pltpu
from jax.sharding import PartitionSpec as P

COUPLING = 0.5
ROWS = 4
EARLY = 3
CROSSING = 10
WINDOW = 1
CHUNKS = 8
PIECES = 2
BLOCK = 256
MESH = pl.DeviceIdType.MESH


def coefficients(code, rows):
    flip = jnp.where(code >= 4, -1.0, 1.0).astype(jnp.float32)
    quarter = code % 4
    cos = jnp.where(quarter == 0, 1.0, jnp.where(quarter == 2, -1.0, 0.0)).astype(jnp.float32)
    sine = jnp.where(quarter == 1, 1.0, jnp.where(quarter == 3, -1.0, 0.0)).astype(jnp.float32)
    real = lax.broadcasted_iota(jnp.int32, (2 * rows, 128), 0) < rows
    return jnp.where(real, cos, cos * flip), jnp.where(real, -sine * flip, sine)


def kernel(
    nx, ny, groups, rows,
    k_hbm, s_hbm, pat_ref, out_ref,
    s_ref, k_ref, give_ref, take_ref, src_ref, coef_ref, sum_ref, in_x, in_y, fin_out, fin_in,
    s_sem, k_sem, hand_send, hand_recv, send_x, send_y, recv_x, recv_y, fin_send, fin_recv,
):
    width = k_ref.shape[-1]
    nk = ny // 2
    cx = lax.axis_index("gx")
    cy = lax.axis_index("gy")
    ck = cy // 2
    core = cy % 2
    load = pltpu.make_async_copy(k_hbm, k_ref.at[core, 0], k_sem)
    load.start()
    load_s = pltpu.make_async_copy(s_hbm, s_ref, s_sem)
    load_s.start()

    last_depth = nx - 1 + 2 * (nk - 1)
    depth = (cx + 2 * ck, last_depth - cx - 2 * ck)
    step_of = (1, -1)
    has_x = (cx > 0, cx < nx - 1)
    has_y = (ck > 0, ck < nk - 1)

    def core_of(parity, side, along):
        mine = depth[side] + along
        gap = 2 * mine - last_depth
        moved = (gap > -CROSSING) & (gap < CROSSING) if side == 0 else gap < -last_depth
        return jnp.where(mine < EARLY, parity, jnp.where(moved, 0, 1))

    here = tuple(tuple(core_of(parity, side, 0) for side in range(2)) for parity in range(2))
    apart = tuple(here[0][side] != here[1][side] for side in range(2))

    barrier = pltpu.get_barrier_semaphore()
    pl.semaphore_signal(barrier, inc=1, device_id=(cx, cy + 1 - 2 * core), device_id_type=MESH)
    for side in range(2):
        back = -step_of[side]

        @pl.when(has_x[side])
        def _():
            for other in range(2):
                pl.semaphore_signal(
                    barrier, inc=1, device_id=(cx + back, 2 * ck + other), device_id_type=MESH
                )

        @pl.when(has_y[side])
        def _():
            for other in range(2):
                pl.semaphore_signal(
                    barrier, inc=1, device_id=(cx, 2 * (ck + back) + other), device_id_type=MESH
                )

    zero = jnp.zeros((groups, 2 * rows, width), jnp.float32)
    for side in range(2):
        @pl.when(jnp.logical_not(has_x[side]))
        def _():
            for parity in range(2):
                in_x[parity, side] = zero

        @pl.when(jnp.logical_not(has_y[side]))
        def _():
            in_y[side, side] = zero

        for parity in range(2):
            sum_ref[parity, side] = zero

    for side in range(2):
        for edge in range(2):
            own, swap = coefficients(pat_ref[side, edge], rows)
            coef_ref[core, side, edge, 0] = own
            coef_ref[core, side, edge, 1] = swap
    load_s.wait()
    full = s_ref[...].astype(jnp.float32)
    for group in range(groups):
        part = slice(group * rows, (group + 1) * rows)
        src_ref[core, group] = jnp.concatenate([full[0, part], full[1, part]], axis=0)

    def transpose(parity):
        def block(index, carry):
            piece = index // (width // BLOCK)
            start = pl.multiple_of((index % (width // BLOCK)) * BLOCK, BLOCK)
            k_ref[parity, 1, piece, :, pl.ds(start, BLOCK)] = k_ref[
                parity, 0, piece, pl.ds(start, BLOCK), :
            ].T
            return carry

        lax.fori_loop(0, 2 * (width // BLOCK), block, 0)

    count = 1 + 2 * sum(jnp.where(flag, 1, 0) for flag in has_x + has_y)
    pl.semaphore_wait(barrier, count)

    def handover(src, dst, slot):
        return pltpu.make_async_remote_copy(
            src_ref=src, dst_ref=dst, send_sem=hand_send.at[slot], recv_sem=hand_recv.at[slot],
            device_id=(cx, 2 * ck + 1 - core), device_id_type=MESH,
        )

    chunk_rows = 2 * width // CHUNKS
    per_half = CHUNKS // 2

    def hand_parts(parity):
        return (
            handover(coef_ref.at[parity], coef_ref.at[parity], 0),
            handover(src_ref.at[parity], src_ref.at[parity], 1),
        )

    def chunk_copy(chunk):
        return handover(give_ref.at[chunk], take_ref.at[chunk], 2 + chunk)

    early = (depth[0] < EARLY, depth[1] < EARLY)
    met = (here[0][0] == 0) & jnp.logical_not(early[0]) | (here[0][1] == 0) & jnp.logical_not(early[1])
    gives = (core == 0) | met
    takes = (core == 1) | met
    unused = (core == 1) & (depth[1] == 0)
    turn_now = jnp.logical_not(unused) & (early[1] | (core == 1) & jnp.logical_not(early[0]))

    @pl.when(gives)
    def _():
        for part in hand_parts(core):
            part.start()

    load.wait()

    @pl.when(turn_now)
    def _():
        transpose(core)

    def give():
        def send(chunk, carry):
            start = pl.multiple_of((chunk % per_half) * chunk_rows, chunk_rows)
            give_ref[chunk] = k_ref[
                core, 0, chunk // per_half, pl.ds(start, chunk_rows), :
            ].astype(jnp.float32)
            chunk_copy(chunk).start()
            return carry

        lax.fori_loop(0, CHUNKS, send, 0)

    def take():
        for part in hand_parts(1 - core):
            part.wait_recv()

        def receive(chunk, carry):
            chunk_copy(chunk).wait_recv()
            start = pl.multiple_of((chunk % per_half) * chunk_rows, chunk_rows)
            k_ref[1 - core, 0, chunk // per_half, pl.ds(start, chunk_rows), :] = take_ref[
                chunk
            ].astype(jnp.bfloat16)
            return carry

        lax.fori_loop(0, CHUNKS, receive, 0)

        @pl.when(jnp.where(core == 0, here[1][1], here[0][1]) == core)
        def _():
            transpose(1 - core)

        @pl.when(jnp.logical_not(turn_now) & (jnp.where(core == 0, here[0][1], here[1][1]) == core))
        def _():
            transpose(core)

    take_step = jnp.where(early[0] | early[1], min(EARLY + groups, last_depth - EARLY), 0)

    piece_width = width // PIECES

    def columns(piece):
        return slice(piece * piece_width, (piece + 1) * piece_width)

    def copy_x(parity, side, group, piece):
        step = step_of[side]
        there = core_of(parity, side, 1)
        slot = group * PIECES + piece
        cut = columns(piece)
        return pltpu.make_async_remote_copy(
            src_ref=sum_ref.at[parity, side, group, :, cut],
            dst_ref=in_x.at[parity, side, group, :, cut],
            send_sem=send_x.at[parity, side, slot], recv_sem=recv_x.at[parity, side, slot],
            device_id=(cx + step, 2 * ck + there), device_id_type=MESH,
        )

    def copy_y(parity, side, group, piece):
        step = step_of[side]
        if parity == side:
            target = (cx, 2 * ck + 1 - core)
        else:
            target = (cx, 2 * (ck + step) + core_of(1 - parity, side, 2))
        slot = group * PIECES + piece
        cut = columns(piece)
        return pltpu.make_async_remote_copy(
            src_ref=sum_ref.at[parity, side, group, :, cut],
            dst_ref=in_y.at[1 - parity, side, group, :, cut],
            send_sem=send_y.at[parity, side, slot], recv_sem=recv_y.at[1 - parity, side, slot],
            device_id=target, device_id_type=MESH,
        )

    def fin_copy(group):
        return pltpu.make_async_remote_copy(
            src_ref=fin_out.at[group], dst_ref=fin_in.at[group],
            send_sem=fin_send.at[group], recv_sem=fin_recv.at[group],
            device_id=(cx, 2 * ck + 1 - core), device_id_type=MESH,
        )

    is_second = (depth[0] >= depth[1], depth[0] < depth[1])
    sends_x = (has_x[1], has_x[0])
    sends_y = (has_y[1], has_y[0])

    def exchanged(value):
        return jnp.concatenate([value[rows:], value[:rows]], axis=0)

    def wide(tile):
        return jnp.concatenate([tile] * (piece_width // 128), axis=1)

    def blended(parity, side, group, piece):
        @pl.when(has_x[side])
        def _():
            copy_x(parity, side, group, piece).wait_recv()

        @pl.when(has_y[side] if parity == side else apart[side])
        def _():
            copy_y(1 - parity, side, group, piece).wait_recv()

        left = in_x[parity, side, group, :, columns(piece)]
        down = in_y[parity, side, group, :, columns(piece)]
        coef = [[wide(coef_ref[parity, side, edge, i]) for i in range(2)] for edge in range(2)]
        blend = (
            (coef[0][0] * left + coef[0][1] * exchanged(left))
            + (coef[1][0] * down + coef[1][1] * exchanged(down))
        )
        real = lax.broadcasted_iota(jnp.int32, blend.shape, 0) < rows
        other = exchanged(blend)
        turned = jnp.where(real, -other, other)
        return blend.astype(jnp.bfloat16), turned.astype(jnp.bfloat16)

    def product(parity, side, factors, piece, cut):
        contract = (((1,), (0,)), ((), ()))
        terms = [
            lax.dot_general(
                factor, k_ref[parity, side, half, columns(piece), cut], contract,
                preferred_element_type=jnp.float32,
            )
            for half, factor in enumerate(factors)
        ]
        return terms[0] + terms[1]

    def launch(parity, side, group, piece):
        first = parity == side
        for wanted, copy in (
            (apart[side] if first else sends_y[side], copy_y), (sends_x[side], copy_x)
        ):
            @pl.when(wanted)
            def _():
                if WINDOW < groups:
                    @pl.when(group >= WINDOW)
                    def _():
                        copy(parity, side, group - WINDOW, piece).wait_send()

                copy(parity, side, group, piece).start()

    def finish(parity, side, group):
        last = is_second[side] | (here[parity][1 - side] != core)

        @pl.when((core != parity) & last)
        def _():
            fin_out[group] = sum_ref[parity, 0, group] + sum_ref[parity, 1, group]
            fin_copy(group).start()

    def begin(parity, side, group):
        for piece in range(PIECES):
            cut = columns(piece)
            update = src_ref[parity, group, :, cut]
            sum_ref[parity, side, group, :, cut] = update
            launch(parity, side, group, piece)

            @pl.when(jnp.logical_not(apart[side]))
            def _():
                in_y[1 - parity, side, group, :, cut] = update

        finish(parity, side, group)

    def advance(parity, side, group):
        first = parity == side
        total = None
        for piece in range(PIECES - 1):
            factors = blended(parity, side, group, piece)
            term = product(parity, side, factors, piece, slice(0, width))
            total = term if total is None else total + term
        factors = blended(parity, side, group, PIECES - 1)
        for piece in range(PIECES):
            cut = columns(piece)
            term = product(parity, side, factors, PIECES - 1, cut)
            if total is not None:
                term = total[:, cut] + term
            update = src_ref[parity, group, :, cut] + COUPLING * term
            sum_ref[parity, side, group, :, cut] = update
            launch(parity, side, group, piece)
            if first:
                @pl.when(jnp.logical_not(apart[side]))
                def _():
                    in_y[1 - parity, side, group, :, cut] = update

        finish(parity, side, group)

    def runs(parity, side):
        return core == here[parity][side]

    def section(step, carry):
        @pl.when(gives & (step == take_step))
        def _():
            give()

        @pl.when(takes & (step == take_step))
        def _():
            take()

        for side in (1, 0):
            group = step - depth[side]
            for parity in (side, 1 - side):
                @pl.when((group >= 0) & (group < groups) & runs(parity, side))
                def _():
                    if parity == side:
                        @pl.when(depth[side] == 0)
                        def _():
                            begin(parity, side, group)

                        @pl.when(depth[side] > 0)
                        def _():
                            advance(parity, side, group)
                    else:
                        advance(parity, side, group)

        return carry

    lax.fori_loop(0, last_depth + groups, section, 0)

    def store(start, parts):
        at = slice(start * rows, (start + len(parts)) * rows)
        for half in range(2):
            out_ref[half, at] = jnp.concatenate(
                [part[half * rows : (half + 1) * rows] for part in parts], axis=0
            ).astype(jnp.bfloat16)

    def any_of(parity, where):
        return (here[parity][0] == where) | (here[parity][1] == where)

    for parity in range(2):
        awaits = any_of(parity, 1 - parity)

        @pl.when((core == parity) & awaits)
        def _():
            per = 16 // rows
            for start in range(0, groups, per):
                block = range(start, start + per)
                for group in block:
                    fin_copy(group).wait_recv()
                store(start, [
                    fin_in[group] + sum_ref[parity, 0, group] + sum_ref[parity, 1, group]
                    for group in block
                ])

        @pl.when((core == parity) & jnp.logical_not(awaits))
        def _():
            store(0, [sum_ref[parity, 0, group] + sum_ref[parity, 1, group] for group in range(groups)])

        @pl.when((core != parity) & awaits)
        def _():
            def sent(group, carry):
                fin_copy(group).wait_send()
                return carry

            lax.fori_loop(0, groups, sent, 0)

    @pl.when(gives)
    def _():
        for part in hand_parts(core):
            part.wait_send()

        def sent(chunk, carry):
            chunk_copy(chunk).wait_send()
            return carry

        lax.fori_loop(0, CHUNKS, sent, 0)

    def drain(group, carry):
        for side in range(2):
            for parity in range(2):
                over = apart[side] if parity == side else sends_y[side]
                for piece in range(PIECES):
                    @pl.when(runs(parity, side) & sends_x[side])
                    def _():
                        copy_x(parity, side, group, piece).wait_send()

                    @pl.when(runs(parity, side) & over)
                    def _():
                        copy_y(parity, side, group, piece).wait_send()

        return carry

    lax.fori_loop(max(0, groups - WINDOW), groups, drain, 0)


def per_device(nx, ny, impedance, sources, pattern):
    _, _, _, count, width = sources.shape
    rows = ROWS
    groups = count // rows
    trace = (2, 2, groups, 2 * rows, width)
    vmem = pl.BlockSpec(memory_space=pltpu.VMEM)
    dma = pltpu.SemaphoreType.DMA
    result = pl.pallas_call(
        functools.partial(kernel, nx, ny, groups, rows),
        out_shape=jax.ShapeDtypeStruct((2, count, width), jnp.bfloat16),
        in_specs=[
            pl.BlockSpec(memory_space=pl.ANY),
            pl.BlockSpec(memory_space=pl.ANY),
            pl.BlockSpec(memory_space=pltpu.SMEM),
        ],
        out_specs=vmem,
        scratch_shapes=[
            pltpu.VMEM((2, count, width), jnp.bfloat16),
            pltpu.VMEM((2, 2, 2, width, width), jnp.bfloat16),
            pltpu.VMEM((CHUNKS, 2 * width // CHUNKS, width), jnp.float32),
            pltpu.VMEM((CHUNKS, 2 * width // CHUNKS, width), jnp.float32),
            pltpu.VMEM((2, groups, 2 * rows, width), jnp.float32),
            pltpu.VMEM((2, 2, 2, 2, 2 * rows, 128), jnp.float32),
            pltpu.VMEM(trace, jnp.float32),
            pltpu.VMEM(trace, jnp.float32),
            pltpu.VMEM(trace, jnp.float32),
            pltpu.VMEM((groups, 2 * rows, width), jnp.float32),
            pltpu.VMEM((groups, 2 * rows, width), jnp.float32),
            dma,
            dma,
            dma((2 + CHUNKS,)),
            dma((2 + CHUNKS,)),
            dma((2, 2, groups * PIECES)),
            dma((2, 2, groups * PIECES)),
            dma((2, 2, groups * PIECES)),
            dma((2, 2, groups * PIECES)),
            dma((groups,)),
            dma((groups,)),
        ],
        compiler_params=pltpu.CompilerParams(
            collective_id=0, has_side_effects=True, vmem_limit_bytes=56 * 1024 * 1024
        ),
    )(impedance[0, 0], sources[0, 0], pattern[0, 0])
    return result[None, None]


def solution(mesh):
    in_specs = (
        P("gx", "gy", None, None, None),
        P("gx", "gy", None, None, None),
        P("gx", "gy", None, None),
    )
    out_specs = P("gx", "gy", None, None, None)
    body = functools.partial(per_device, mesh.shape["gx"], mesh.shape["gy"])
    return jax.shard_map(body, mesh=mesh, in_specs=in_specs, out_specs=out_specs, check_vma=False)
```
